256 devices in a mesh: section: 4 (over x_lo, core), dp: 16 (over z, x_hi), fsdp: 4 (over y).
Axes of the slice: x: 4 (x_hi: 2, x_lo: 2; x = x_hi * 2 + x_lo), y: 4, z: 8, core: 2. Of those that a mesh axis runs over, the one named last changes fastest.
Arguments:
- saved_input: bfloat16 [4, 2048, 3072], P('section', 'dp', 'fsdp'), may hold values from -6 to 6
- pending_grad: bfloat16 [4, 2048, 3072], P('section', 'dp', 'fsdp'), may hold values from -6 to 6
- gate_pre: bfloat16 [4, 2048, 8192], P('section', None, ('dp', 'fsdp')), may hold values from -6 to 6
- up_pre: bfloat16 [4, 2048, 8192], P('section', None, ('dp', 'fsdp')), may hold values from -6 to 6
- block_expert: int32 [4, 16], P('section', 'dp'), may hold values from 0 to 2
- gate_weight: bfloat16 [4, 2, 3072, 8192], P('section', None, 'fsdp', 'dp'), may hold values from -0.109375 to 0.109375
- up_weight: bfloat16 [4, 2, 3072, 8192], P('section', None, 'fsdp', 'dp'), may hold values from -0.109375 to 0.109375
- down_weight: bfloat16 [4, 2, 8192, 3072], P('section', None, 'dp', 'fsdp'), may hold values from -0.0625 to 0.0625
Outputs:
- input_grad: bfloat16 [4, 2048, 3072], P('section', 'dp', 'fsdp')
- gate_weight_grad: bfloat16 [4, 2, 3072, 8192], P('section', None, 'fsdp', 'dp')
- up_weight_grad: bfloat16 [4, 2, 3072, 8192], P('section', None, 'fsdp', 'dp')
- down_weight_grad: bfloat16 [4, 2, 8192, 3072], P('section', None, 'dp', 'fsdp')
The draws below stay inside these ranges and needn't reach their ends.
Inputs may be any that keep to these rules, and one draw needn't show every extreme that they name: `block_expert`: the value 2 marks a block of padding rows; any other value names the block's expert.
All inputs are finite; a program needn't handle non-finite values.
Results may differ from the reference program's by a relative error of at most 0.0049.
Values may be sent and summed in bfloat16 or wider, within the bound.
No kernel may reach another device: no remote copies, remote signals or barrier semaphores. Data moves between devices by JAX's collectives and lax.ppermute only.
A program may use at most 128 MiB of HBM per device.

```python
import math
import jax
import jax.numpy as jnp

D = 3072
FF = 8192
E = 2
BLOCK = 128
TOKENS = 2048
N_SECTION = 4


def touch_ends(values, stream_key, low, largest):
    index_at = [jax.random.randint(jax.random.fold_in(stream_key, axis), (), 0, length) for axis, length in enumerate(values.shape)]
    longest = values.shape.index(max(values.shape))
    neighbour = index_at[:longest] + [(index_at[longest] + 1) % values.shape[longest]] + index_at[longest + 1:]
    return values.at[tuple(index_at)].set(low).at[tuple(neighbour)].set(largest)


def steps_of(own_key, shape, pieces, smallest, high):
    factor_of = 1.0
    for position, shards_of in pieces:
        steps = jax.random.uniform(jax.random.fold_in(jax.random.fold_in(own_key, 6), position), (shards_of,), jnp.float32, smallest / len(pieces), high / len(pieces))
        factor_of = factor_of * jnp.repeat(jnp.exp(steps), shape[position] // shards_of).reshape((-1,) + (1,) * (len(shape) - 1 - position))
    return factor_of


def centred(rng, dims, scale, reach, split=(), dtype=jnp.bfloat16):
    values = scale * jax.random.normal(rng, dims, jnp.float32)
    if split:
        values = values * steps_of(rng, dims, split, -0.22, 0.18)
    return jnp.clip(values, -reach, reach).astype(dtype)


def setup_inputs(seed: int = 0) -> dict:
    key_list = jax.random.split(jax.random.key(seed), 9)
    saved_input = centred(key_list[0], (N_SECTION, TOKENS, D), 1.0, 6.0, ((0, 4), (1, 16), (2, 4)))
    pending_grad = centred(key_list[1], (N_SECTION, TOKENS, D), 1.0, 6.0, ((0, 4), (1, 16), (2, 4)))
    gate_pre = centred(key_list[2], (N_SECTION, TOKENS, FF), 1.0, 6.0, ((0, 4), (2, 64)))
    up_pre = centred(key_list[3], (N_SECTION, TOKENS, FF), 1.0, 6.0, ((0, 4), (2, 64)))
    block_expert = touch_ends(jax.random.randint(key_list[4], (N_SECTION, TOKENS // BLOCK), 0, E + 1), jax.random.fold_in(key_list[4], 1), 0, E).astype(jnp.int32)
    gate_weight = centred(key_list[5], (N_SECTION, E, D, FF), D ** -0.5, 0.109375, ((0, 4), (2, 4), (3, 16)))
    up_weight = centred(key_list[6], (N_SECTION, E, D, FF), D ** -0.5, 0.109375, ((0, 4), (2, 4), (3, 16)))
    down_weight = centred(key_list[7], (N_SECTION, E, FF, D), FF ** -0.5, 0.0625, ((0, 4), (2, 16), (3, 4)))
    return {"saved_input": saved_input, "pending_grad": pending_grad, "gate_pre": gate_pre, "up_pre": up_pre, "block_expert": block_expert, "gate_weight": gate_weight, "up_weight": up_weight, "down_weight": down_weight}


def swiglu_back(hidden_grad, gate_pre, up_pre):
    gate_value = gate_pre.astype(jnp.float32)
    up_value = up_pre.astype(jnp.float32)
    sigmoid_gate = jax.nn.sigmoid(gate_value)
    active = gate_value * sigmoid_gate
    hidden = (active * up_value).astype(jnp.bfloat16)
    gate_grad = (hidden_grad * up_value * sigmoid_gate * (1.0 + gate_value * (1.0 - sigmoid_gate))).astype(jnp.bfloat16)
    up_grad = (hidden_grad * active).astype(jnp.bfloat16)
    return (hidden, gate_grad, up_grad)

def section_backward(inputs, cotangent, gate_pre, up_pre, experts, gate_weight, up_weight, down_weight):
    token_count = inputs.shape[0]
    per_row = jnp.repeat(experts, BLOCK)
    grad_scale = 1.0 / math.sqrt(token_count)
    hidden_grad = jnp.zeros((token_count, FF), jnp.float32)
    route_masks = []
    for expert in range(E):
        route_mask = (per_row == expert).astype(jnp.float32)[:, None]
        route_masks.append(route_mask)
        hidden_grad = hidden_grad + route_mask * jnp.dot(cotangent, down_weight[expert].T, preferred_element_type=jnp.float32)
    hidden, gate_grad, up_grad = swiglu_back(hidden_grad, gate_pre, up_pre)
    input_grad = jnp.zeros((token_count, D), jnp.float32)
    gate_list = []
    up_list = []
    down_list = []
    for expert in range(E):
        weight_mask = route_masks[expert].astype(jnp.bfloat16)
        gate_list.append((jnp.dot(inputs.T, gate_grad * weight_mask, preferred_element_type=jnp.float32) * grad_scale).astype(jnp.bfloat16))
        up_list.append((jnp.dot(inputs.T, up_grad * weight_mask, preferred_element_type=jnp.float32) * grad_scale).astype(jnp.bfloat16))
        down_list.append((jnp.dot((hidden * weight_mask).T, cotangent, preferred_element_type=jnp.float32) * grad_scale).astype(jnp.bfloat16))
        branch = jnp.dot(gate_grad, gate_weight[expert].T, preferred_element_type=jnp.float32) + jnp.dot(up_grad, up_weight[expert].T, preferred_element_type=jnp.float32)
        input_grad = input_grad + route_masks[expert] * branch
    return (input_grad.astype(jnp.bfloat16), jnp.stack(gate_list), jnp.stack(up_list), jnp.stack(down_list))

def reference(saved_input, pending_grad, gate_pre, up_pre, block_expert, gate_weight, up_weight, down_weight):
    results = []
    for section_index in range(N_SECTION):
        following = (section_index + 1) % N_SECTION
        results.append(section_backward(saved_input[section_index], pending_grad[following], gate_pre[section_index], up_pre[section_index], block_expert[section_index], gate_weight[section_index], up_weight[section_index], down_weight[section_index]))
    return (jnp.stack([result[0] for result in results]), jnp.stack([result[1] for result in results]), jnp.stack([result[2] for result in results]), jnp.stack([result[3] for result in results]))
```

```python
import functools
import math

import jax
import jax.numpy as jnp
from jax import lax
from jax.experimental import pallas as pl
from jax.experimental.pallas import tpu as pltpu
from jax.sharding import Mesh
from jax.sharding import PartitionSpec as P

E = 2
BLOCK = 128
TAG = 16
VMEM_LIMIT = 56 * 1024 * 1024
NT = (((1,), (1,)), ((), ()))
VM = pl.BlockSpec(memory_space=pltpu.VMEM)
SM = pl.BlockSpec(memory_space=pltpu.SMEM)
F32 = jnp.float32
BF16 = jnp.bfloat16


def shifted(x, axis, by):
    count = lax.axis_size(axis)
    return lax.ppermute(x, axis, [(i, (i + by) % count) for i in range(count)])


def block_rows(index):
    return pl.ds(pl.multiple_of(index * BLOCK, BLOCK), BLOCK)


def kernel_call(body, out_shape, in_specs, out_specs, scratch, flops, size):
    return pl.pallas_call(
        body,
        out_shape=out_shape,
        in_specs=in_specs,
        out_specs=out_specs,
        scratch_shapes=scratch,
        compiler_params=pltpu.CompilerParams(vmem_limit_bytes=VMEM_LIMIT),
        cost_estimate=pl.CostEstimate(flops=flops, bytes_accessed=size, transcendentals=0),
    )


def hidden_body(count, groups, place_ref, *refs):
    pieces = refs[:count]
    weight_ref = refs[count]
    parts = refs[count + 1 : count + 1 + groups]
    expert_ref = refs[count + 1 + groups]
    turned = refs[count + 2 + groups]
    width = weight_ref.shape[1] // groups
    y = place_ref[0]
    for expert in range(E):
        for k in range(groups):
            group = lax.rem(y + k, groups)
            turned[expert, k * width : (k + 1) * width, :] = weight_ref[
                expert, pl.ds(pl.multiple_of(group * width, width), width), :
            ]
    for j in range(count):
        tag = jnp.max(pieces[j][BLOCK : BLOCK + TAG, 0:128].astype(F32))
        expert = tag.astype(jnp.int32)
        expert_ref[j] = expert
        valid = (expert < E).astype(F32)
        product = lax.dot_general(
            pieces[j][0:BLOCK, :],
            turned[jnp.minimum(expert, E - 1)],
            NT,
            preferred_element_type=F32,
        )
        product = product * valid
        for k in range(groups):
            parts[k][j * BLOCK : (j + 1) * BLOCK, :] = product[
                :, k * width : (k + 1) * width
            ].astype(parts[k].dtype)


def hidden_part(place, pieces, weight, groups):
    count = len(pieces)
    rows = count * BLOCK
    hidden, cols = weight.shape[1:]
    width = hidden // groups
    out_shape = [jax.ShapeDtypeStruct((rows, width), F32 if k == 0 else BF16) for k in range(groups)]
    out_shape.append(jax.ShapeDtypeStruct((count,), jnp.int32))
    outs = kernel_call(
        functools.partial(hidden_body, count, groups),
        out_shape,
        [SM] + [VM] * (count + 1),
        [VM] * groups + [SM],
        [pltpu.VMEM(weight.shape, BF16)],
        2 * rows * hidden * cols,
        2 * (rows * cols + E * hidden * cols + rows * hidden),
    )(place, *pieces, weight)
    return outs[:groups], outs[groups]


def back_body(plan, groups, place_ref, ids_ref, expert_ref, *refs):
    grads = refs[:groups]
    saved = refs[groups : 2 * groups]
    gate_w, up_w = refs[2 * groups : 2 * groups + 2]
    hidden_ref, gate_ref, up_ref = refs[2 * groups + 2 : 2 * groups + 5]
    outs = refs[2 * groups + 5 :]
    width = grads[0].shape[1]
    y = place_ref[0]
    for j, (slot, offset) in enumerate(plan):
        rows = slice(j * BLOCK, (j + 1) * BLOCK)
        saved_rows = block_rows(ids_ref[j])
        for k in range(groups):
            group = lax.rem(y + groups - k, groups)
            cols = pl.ds(pl.multiple_of(group * width, width), width)
            grad = grads[k][rows, :].astype(F32)
            gate = saved[k][saved_rows, 0:width].astype(F32)
            up = saved[k][saved_rows, width : 2 * width].astype(F32)
            sig = 1.0 / (1.0 + jnp.exp(-gate))
            active = gate * sig
            hidden_ref[rows, cols] = (active * up).astype(BF16)
            gate_ref[rows, cols] = (grad * up * sig * (1.0 + gate * (1.0 - sig))).astype(BF16)
            up_ref[rows, cols] = (grad * active).astype(BF16)
        chosen = jnp.minimum(expert_ref[j], E - 1)
        share = lax.dot_general(gate_ref[rows, :], gate_w[chosen], NT, preferred_element_type=F32)
        share = share + lax.dot_general(
            up_ref[rows, :], up_w[chosen], NT, preferred_element_type=F32
        )
        outs[slot][offset * BLOCK : (offset + 1) * BLOCK, :] = share.astype(outs[slot].dtype)


def back_part(place, ids, experts, grads, saved, gate_w, up_w, plan, slots):
    groups = len(grads)
    rows = len(plan) * BLOCK
    cols, hidden = gate_w.shape[1:]
    out_shape = [jax.ShapeDtypeStruct((rows, hidden), BF16)] * 3
    out_shape += [jax.ShapeDtypeStruct((blocks * BLOCK, cols), kind) for blocks, kind in slots]
    outs = kernel_call(
        functools.partial(back_body, plan, groups),
        out_shape,
        [SM] * 3 + [VM] * (2 * groups + 2),
        [VM] * len(out_shape),
        [],
        4 * rows * hidden * cols,
        2 * (2 * E * hidden * cols + 6 * rows * hidden + 2 * rows * cols),
    )(place, ids, experts, *grads, *saved, gate_w, up_w)
    return outs[:3], outs[3:]


def weight_body(counts, scale, ids_ref, *refs):
    chunks = len(counts)
    total = sum(counts)
    experts = refs[:chunks]
    x_ref = refs[chunks]
    pieces = refs[chunks + 1 : chunks + 1 + total]
    base = chunks + 1 + total
    acts = [refs[base + 3 * c : base + 3 * c + 3] for c in range(chunks)]
    base += 3 * chunks
    gate_out, up_out, down_out = refs[base : base + 3]
    x_t, h_t, c_s, gate_s, up_s, gate_acc, up_acc, down_acc = refs[base + 3 :]
    slots = total + 2

    def put(slot, x, hidden, cot, gate, up):
        at = block_rows(slot)
        x_t[:, at] = x.T
        h_t[:, at] = hidden.T
        c_s[at, :] = cot
        gate_s[at, :] = gate
        up_s[at, :] = up

    seen = [jnp.int32(0), jnp.int32(0)]
    j = 0
    for c in range(chunks):
        for i in range(counts[c]):
            expert = experts[c][i]
            first = (expert == 0).astype(jnp.int32)
            second = (expert == 1).astype(jnp.int32)
            slot = jnp.where(expert == 0, seen[0], slots - 1 - seen[1])

            @pl.when(expert < E)
            def _(c=c, i=i, j=j, slot=slot):
                rows = slice(i * BLOCK, (i + 1) * BLOCK)
                hidden_ref, gate_ref, up_ref = acts[c]
                put(
                    slot,
                    x_ref[block_rows(ids_ref[j]), :],
                    hidden_ref[rows, :],
                    pieces[j][0:BLOCK, :],
                    gate_ref[rows, :],
                    up_ref[rows, :],
                )

            seen = [seen[0] + first, seen[1] + second]
            j += 1

    for slot, odd in (
        (seen[0], lax.rem(seen[0], 2)),
        (slots - 1 - seen[1], lax.rem(seen[1], 2)),
    ):

        @pl.when(odd == 1)
        def _(slot=slot):
            at = block_rows(slot)
            for ref in (x_t, h_t):
                ref[:, at] = jnp.zeros((ref.shape[0], BLOCK), BF16)
            for ref in (c_s, gate_s, up_s):
                ref[at, :] = jnp.zeros((BLOCK, ref.shape[1]), BF16)

    for expert in range(E):
        for acc in (gate_acc, up_acc, down_acc):
            acc[...] = jnp.zeros(acc.shape, F32)
        pairs = lax.div(seen[expert] + 1, 2)

        def add(step, carry, expert=expert):
            pair = step if expert == 0 else slots // 2 - 1 - step
            at = pl.ds(pl.multiple_of(pair * (2 * BLOCK), 2 * BLOCK), 2 * BLOCK)
            x = x_t[:, at]
            gate_acc[...] += jnp.dot(x, gate_s[at, :], preferred_element_type=F32)
            up_acc[...] += jnp.dot(x, up_s[at, :], preferred_element_type=F32)
            down_acc[...] += jnp.dot(h_t[:, at], c_s[at, :], preferred_element_type=F32)
            return carry

        lax.fori_loop(0, pairs, add, 0)
        gate_out[expert] = (gate_acc[...] * scale).astype(BF16)
        up_out[expert] = (up_acc[...] * scale).astype(BF16)
        down_out[expert] = (down_acc[...] * scale).astype(BF16)


def weight_part(ids, experts, x, pieces, acts, scale):
    counts = tuple(a[0].shape[0] // BLOCK for a in acts)
    total = sum(counts)
    rows, cols = x.shape
    hidden = acts[0][0].shape[1]
    wide = (total + 2) * BLOCK
    return kernel_call(
        functools.partial(weight_body, counts, scale),
        [
            jax.ShapeDtypeStruct((E, cols, hidden), BF16),
            jax.ShapeDtypeStruct((E, cols, hidden), BF16),
            jax.ShapeDtypeStruct((E, hidden, cols), BF16),
        ],
        [SM] * (1 + len(counts)) + [VM] * (1 + total + 3 * len(counts)),
        [VM] * 3,
        [
            pltpu.VMEM((cols, wide), BF16),
            pltpu.VMEM((hidden, wide), BF16),
            pltpu.VMEM((wide, cols), BF16),
            pltpu.VMEM((wide, hidden), BF16),
            pltpu.VMEM((wide, hidden), BF16),
            pltpu.VMEM((cols, hidden), F32),
            pltpu.VMEM((cols, hidden), F32),
            pltpu.VMEM((hidden, cols), F32),
        ],
        6 * rows * cols * hidden,
        2 * (2 * rows * cols + 3 * rows * hidden + 3 * E * cols * hidden),
    )(ids, *experts, x, *pieces, *[ref for act in acts for ref in act])


def local(
    saved_input, pending_grad, gate_pre, up_pre, block_expert, gate_weight, up_weight, down_weight
):
    nz = lax.axis_size("z")
    groups = lax.axis_size("fsdp")
    z, xh, y = lax.axis_index("z"), lax.axis_index("xh"), lax.axis_index("fsdp")
    place = jnp.stack([y, z, xh]).astype(jnp.int32)
    half = nz // 2

    cotangent = shifted(pending_grad[0], "section", -1)
    tag = jnp.broadcast_to(block_expert.astype(BF16), (TAG, cotangent.shape[1]))
    own = jnp.concatenate([cotangent, tag], axis=0)
    across = lambda v: shifted(v, "xh", 1)

    pieces = {0: (own, across(own))}
    up_going = down_going = own
    for d in range(1, half):
        up_going = shifted(up_going, "z", 1)
        down_going = shifted(down_going, "z", -1)
        pieces[-d] = (up_going, across(up_going))
        pieces[d] = (down_going, across(down_going))
    up_going = shifted(up_going, "z", 1)
    pieces[half] = (up_going, across(up_going))

    saved = jnp.concatenate([gate_pre[0], up_pre[0]], axis=1)
    saved_all = [saved] + [shifted(saved, "fsdp", k) for k in range(1, groups)]

    x = saved_input[0]
    x, _ = lax.optimization_barrier((x, up_going))
    x_other = across(x)
    x_pair = jnp.where(
        xh == 0, jnp.concatenate([x, x_other], axis=0), jnp.concatenate([x_other, x], axis=0)
    )
    x_all = lax.all_gather(x_pair, "z", axis=0, tiled=True)

    near = [0] + [s * d for d in range(1, half - 1) for s in (-1, 1)]
    far = [half] + [s * (half - 1) for s in (-1, 1)]
    chunks = (near, far)

    gate_w, up_w, down_w = gate_weight[0], up_weight[0], down_weight[0]
    scale = 1.0 / math.sqrt(saved_input.shape[1] * nz * lax.axis_size("xh"))

    sent = []
    for dists in chunks:
        blocks = [b for d in dists for b in pieces[d]]
        ids = jnp.stack(
            [lax.rem(z + (d + nz), nz) * 2 + h for d in dists for h in (xh, 1 - xh)]
        ).astype(jnp.int32)
        parts, experts = hidden_part(place, blocks, down_w, groups)
        sent.append((blocks, ids, experts, parts))
    summed = []
    for blocks, ids, experts, parts in sent:
        total = parts[0]
        for k in range(1, groups):
            total = total + shifted(parts[k], "fsdp", k).astype(F32)
        summed.append(total)
    grads = []
    for total in summed:
        rounded = total.astype(BF16)
        grads.append([total] + [shifted(rounded, "fsdp", k) for k in range(1, groups)])

    shares = {}
    acts = [None] * len(chunks)
    for c in (1, 0):
        dists = chunks[c]
        blocks, ids, experts, parts = sent[c]
        plan, slots = [], []
        for d in dists:
            slots += [(1, F32), (1, BF16)]
            plan += [(len(slots) - 2, 0), (len(slots) - 1, 0)]
        acts[c], outs = back_part(
            place, ids, experts, grads[c], saved_all, gate_w, up_w, tuple(plan), tuple(slots)
        )
        for i, d in enumerate(dists):
            shares[d] = (outs[2 * i], outs[2 * i + 1])

    def column(d):
        mine, other = shares[d]
        return mine + across(other).astype(F32)

    up_sum = column(half)
    down_sum = None
    for d in range(half - 1, 0, -1):
        up_sum = shifted(up_sum, "z", 1) + column(d)
        arrived = column(-d)
        down_sum = arrived if down_sum is None else shifted(down_sum, "z", -1) + arrived
    input_grad = column(0) + shifted(up_sum, "z", 1) + shifted(down_sum, "z", -1)

    gate_grad, up_grad, down_grad = weight_part(
        jnp.concatenate([sent[0][1], sent[1][1]]),
        [sent[0][2], sent[1][2]],
        x_all,
        sent[0][0] + sent[1][0],
        acts,
        scale,
    )
    return (input_grad.astype(BF16)[None], gate_grad[None], up_grad[None], down_grad[None])


def solution(mesh):
    sizes = mesh.shape
    split = Mesh(
        mesh.devices.reshape(sizes["section"], sizes["dp"] // 2, 2, sizes["fsdp"]),
        ("section", "z", "xh", "fsdp"),
    )
    dp = ("z", "xh")
    rows = P("section", dp, "fsdp")
    kept = P("section", None, ("z", "xh", "fsdp"))
    wide = P("section", None, "fsdp", dp)
    tall = P("section", None, dp, "fsdp")
    return jax.shard_map(
        local,
        mesh=split,
        in_specs=(rows, rows, kept, kept, P("section", dp), wide, wide, tall),
        out_specs=(rows, wide, wide, tall),
        check_vma=False,
    )
```

```python
import functools
import math

import jax
import jax.numpy as jnp
from jax import lax
from jax.experimental import pallas as pl
from jax.experimental.pallas import tpu as pltpu
from jax.sharding import Mesh
from jax.sharding import PartitionSpec as P

E = 2
BLOCK = 128
TAG = 16
VMEM_LIMIT = 60 << 20
NT = (((1,), (1,)), ((), ()))
VM = pl.BlockSpec(memory_space=pltpu.VMEM)
SM = pl.BlockSpec(memory_space=pltpu.SMEM)
F32 = jnp.float32
BF16 = jnp.bfloat16


def shifted(x, axis, by):
    count = lax.axis_size(axis)
    return lax.ppermute(x, axis, [(i, (i + by) % count) for i in range(count)])


def aligned(index, size):
    return pl.ds(pl.multiple_of(index * size, size), size)


def kernel_call(body, out_shape, in_specs, out_specs, scratch, flops, size):
    return pl.pallas_call(
        body,
        out_shape=out_shape,
        in_specs=in_specs,
        out_specs=out_specs,
        scratch_shapes=scratch,
        compiler_params=pltpu.CompilerParams(vmem_limit_bytes=VMEM_LIMIT),
        cost_estimate=pl.CostEstimate(flops=flops, bytes_accessed=size, transcendentals=0),
    )


def piece_of(pieces, j):
    step = BLOCK + TAG
    for piece in pieces:
        held = piece.shape[0] // step
        if j < held:
            start = j * step
            return piece[start : start + BLOCK, :], piece[start + BLOCK : start + step, 0:128]
        j -= held


def hidden_body(count, groups, place_ref, weight_ref, *refs):
    pieces, parts = refs[: -groups - 2], refs[-groups - 2 : -2]
    expert_ref, turned = refs[-2:]
    width = weight_ref.shape[1] // groups
    y = place_ref[0]
    for expert in range(E):
        for k in range(groups):
            turned[expert, k * width : (k + 1) * width, :] = weight_ref[
                expert, aligned(lax.rem(y + k, groups), width), :
            ]
    for j in range(count):
        rows, tag = piece_of(pieces, j)
        expert = jnp.max(tag.astype(F32)).astype(jnp.int32)
        expert_ref[j] = expert
        product = lax.dot_general(
            rows, turned[jnp.minimum(expert, E - 1)], NT, preferred_element_type=F32
        )
        product = product * (expert < E).astype(F32)
        for k in range(groups):
            parts[k][j * BLOCK : (j + 1) * BLOCK, :] = product[
                :, k * width : (k + 1) * width
            ].astype(parts[k].dtype)


def hidden_part(place, pieces, weight, groups):
    count = sum(piece.shape[0] for piece in pieces) // (BLOCK + TAG)
    rows = count * BLOCK
    hidden, cols = weight.shape[1:]
    out_shape = [
        jax.ShapeDtypeStruct((rows, hidden // groups), F32 if k == 0 else BF16)
        for k in range(groups)
    ]
    out_shape.append(jax.ShapeDtypeStruct((count,), jnp.int32))
    outs = kernel_call(
        functools.partial(hidden_body, count, groups),
        out_shape,
        [SM] + [VM] * (len(pieces) + 1),
        [VM] * groups + [SM],
        [pltpu.VMEM(weight.shape, BF16)],
        2 * rows * hidden * cols,
        2 * (rows * cols + E * hidden * cols + rows * hidden),
    )(place, weight, *pieces)
    return outs[:groups], outs[groups]


def saved_pair(saved, k, rows):
    first, second, third, gate_ref, up_ref = saved
    if k == 2:
        gate, up = gate_ref[rows, :].astype(F32), up_ref[rows, :].astype(F32)
    else:
        both = (first, second, None, third)[k][rows, :].astype(F32)
        width = both.shape[1] // 2
        gate, up = both[:, :width], both[:, width:]
    return gate, up, 1.0 / (1.0 + jnp.exp(-gate))


def back_body(first, splits, groups, place_ref, ids_ref, expert_ref, *refs):
    grads, saved = refs[:groups], refs[groups : groups + 5]
    gate_w, up_w, gate_ref, up_ref = refs[groups + 5 : groups + 9]
    outs = refs[groups + 9 :]
    width = grads[0].shape[1]
    y = place_ref[0]
    out_at = [(out, i) for out, blocks in zip(outs, splits) for i in range(blocks)]
    for j, (out, i) in enumerate(out_at):
        rows = slice(j * BLOCK, (j + 1) * BLOCK)
        at = first + j
        saved_rows = aligned(ids_ref[at], BLOCK)
        for k in range(groups):
            cols = aligned(lax.rem(y + groups - k, groups), width)
            grad = grads[k][at * BLOCK : (at + 1) * BLOCK, :].astype(F32)
            gate, up, sig = saved_pair(saved, k, saved_rows)
            gate_ref[rows, cols] = (grad * up * sig * (1.0 + gate * (1.0 - sig))).astype(BF16)
            up_ref[rows, cols] = (grad * (gate * sig)).astype(BF16)
        chosen = jnp.minimum(expert_ref[at], E - 1)
        share = lax.dot_general(gate_ref[rows, :], gate_w[chosen], NT, preferred_element_type=F32)
        share = share + lax.dot_general(
            up_ref[rows, :], up_w[chosen], NT, preferred_element_type=F32
        )
        out[i * BLOCK : (i + 1) * BLOCK, :] = share.astype(out.dtype)


def back_part(place, ids, experts, grads, saved, gate_w, up_w, first, splits, kind):
    groups = len(grads)
    rows = sum(splits) * BLOCK
    cols, hidden = gate_w.shape[1:]
    out_shape = [jax.ShapeDtypeStruct((rows, hidden), BF16)] * 2
    out_shape += [jax.ShapeDtypeStruct((blocks * BLOCK, cols), kind) for blocks in splits]
    outs = kernel_call(
        functools.partial(back_body, first, splits, groups),
        out_shape,
        [SM] * 3 + [VM] * (groups + 7),
        [VM] * len(out_shape),
        [],
        4 * rows * hidden * cols,
        2 * (2 * E * hidden * cols + 6 * rows * hidden + 2 * rows * cols),
    )(place, ids, experts, *grads, *saved, gate_w, up_w)
    return outs[:2], outs[2:]


def weight_body(scale, put, experts, outs, lhs_t, rhs_s, accs):
    slots = sum(ref.shape[0] for ref in experts) + 2
    seen = [jnp.int32(0), jnp.int32(0)]
    for c, ref in enumerate(experts):
        for i in range(ref.shape[0]):
            expert = ref[i]
            slot = jnp.where(expert == 0, seen[0], slots - 1 - seen[1])

            @pl.when(expert < E)
            def _(c=c, i=i, slot=slot):
                put(c, i, aligned(slot, BLOCK))

            seen = [seen[e] + (expert == e).astype(jnp.int32) for e in range(E)]

    for slot, odd in (
        (seen[0], lax.rem(seen[0], 2)),
        (slots - 1 - seen[1], lax.rem(seen[1], 2)),
    ):

        @pl.when(odd == 1)
        def _(slot=slot):
            at = aligned(slot, BLOCK)
            lhs_t[:, at] = jnp.zeros((lhs_t.shape[0], BLOCK), BF16)
            for ref in rhs_s:
                ref[at, :] = jnp.zeros((BLOCK, ref.shape[1]), BF16)

    for expert in range(E):
        for acc in accs:
            acc[...] = jnp.zeros(acc.shape, F32)

        def add(step, carry, expert=expert):
            pair = step if expert == 0 else slots // 2 - 1 - step
            at = aligned(pair, 2 * BLOCK)
            lhs = lhs_t[:, at]
            for acc, rhs in zip(accs, rhs_s):
                acc[...] += jnp.dot(lhs, rhs[at, :], preferred_element_type=F32)
            return carry

        lax.fori_loop(0, lax.div(seen[expert] + 1, 2), add, 0)
        for out, acc in zip(outs, accs):
            out[expert] = (acc[...] * scale).astype(BF16)


def in_weight_body(scale, ids_ref, *refs):
    experts, x_ref, gates, ups, outs = refs[0:2], refs[2], refs[3:6], refs[6:9], refs[9:11]
    lhs_t, gate_s, up_s, gate_acc, up_acc = refs[11:]
    first = experts[0].shape[0]
    early = gates[1].shape[0] // BLOCK

    def put(c, i, at):
        j = i
        if c == 1 and i >= early:
            c, j = 2, i - early
        rows = slice(j * BLOCK, (j + 1) * BLOCK)
        lhs_t[:, at] = x_ref[aligned(ids_ref[min(c, 1) * first + i], BLOCK), :].T
        gate_s[at, :] = gates[c][rows, :]
        up_s[at, :] = ups[c][rows, :]

    weight_body(scale, put, experts, outs, lhs_t, [gate_s, up_s], [gate_acc, up_acc])


def in_weights(ids, experts, x, gates, ups, scale):
    rows, cols = x.shape
    hidden = gates[0].shape[1]
    wide = rows + 2 * BLOCK
    return kernel_call(
        functools.partial(in_weight_body, scale),
        [jax.ShapeDtypeStruct((E, cols, hidden), BF16)] * 2,
        [SM] * 3 + [VM] * 7,
        [VM] * 2,
        [
            pltpu.VMEM((cols, wide), BF16),
            pltpu.VMEM((wide, hidden), BF16),
            pltpu.VMEM((wide, hidden), BF16),
            pltpu.VMEM((cols, hidden), F32),
            pltpu.VMEM((cols, hidden), F32),
        ],
        4 * rows * cols * hidden,
        2 * (rows * cols + 2 * rows * hidden + 2 * E * cols * hidden),
    )(ids, *experts, x, *gates, *ups)


def down_weight_body(groups, scale, place_ref, ids_ref, *refs):
    experts, saved, pieces = refs[0:2], refs[2:7], refs[7:-4]
    first = experts[0].shape[0]
    out, lhs_t, rhs_s, acc = refs[-4:]
    width = saved[-1].shape[1]
    y = place_ref[0]

    def put(c, i, at):
        rows = aligned(ids_ref[c * first + i], BLOCK)
        for k in range(groups):
            gate, up, sig = saved_pair(saved, k, rows)
            hidden = ((gate * sig) * up).astype(BF16)
            lhs_t[aligned(lax.rem(y + groups - k, groups), width), at] = hidden.T
        rhs_s[at, :] = piece_of(pieces, c * first + i)[0]

    weight_body(scale, put, experts, [out], lhs_t, [rhs_s], [acc])


def down_weights(place, ids, experts, saved, pieces, groups, scale):
    rows, cols = saved[0].shape[0], pieces[0].shape[1]
    width = groups * saved[-1].shape[1]
    wide = rows + 2 * BLOCK
    return kernel_call(
        functools.partial(down_weight_body, groups, scale),
        jax.ShapeDtypeStruct((E, width, cols), BF16),
        [SM] * 4 + [VM] * (5 + len(pieces)),
        VM,
        [
            pltpu.VMEM((width, wide), BF16),
            pltpu.VMEM((wide, cols), BF16),
            pltpu.VMEM((width, cols), F32),
        ],
        2 * rows * cols * width,
        2 * (rows * cols + 2 * rows * width + E * cols * width),
    )(place, ids, *experts, *saved, *pieces)


def local(
    saved_input, pending_grad, gate_pre, up_pre, block_expert, gate_weight, up_weight, down_weight
):
    nz = lax.axis_size("z")
    groups = lax.axis_size("fsdp")
    z, xh, y = lax.axis_index("z"), lax.axis_index("xh"), lax.axis_index("fsdp")
    place = y.astype(jnp.int32).reshape(1)
    half = nz // 2
    join = lax.optimization_barrier
    across = lambda v: shifted(v, "xh", 1)
    gate_w, up_w, down_w = gate_weight[0], up_weight[0], down_weight[0]
    scale = 1.0 / math.sqrt(saved_input.shape[1] * nz * lax.axis_size("xh"))
    order = (half,) + tuple(s * d for d in range(half - 1, 0, -1) for s in (1, -1)) + (0,)
    splits = (1,) + (2,) * (half - 2) + (3,)

    def ids_of(column):
        return jnp.stack([lax.rem(z + (d + nz), nz) * 2 + column for d in order]).astype(jnp.int32)

    mine_ids, other_ids = ids_of(xh), ids_of(1 - xh)
    ids = jnp.concatenate([mine_ids, other_ids])

    def summed(parts, got):
        total = parts[0]
        for part in got:
            total = total + part.astype(F32)
        return total

    def to_others(parts):
        return [shifted(parts[k], "fsdp", k) for k in range(1, groups)]

    def spread(total):
        rounded = total.astype(BF16)
        return [total] + to_others([rounded] * groups)

    cotangent = shifted(pending_grad[0], "section", -1)
    tag = jnp.broadcast_to(block_expert.astype(BF16), (TAG, cotangent.shape[1]))
    own = jnp.concatenate([cotangent, tag], axis=0)
    pair = jnp.concatenate([gate_pre[0], up_pre[0]], axis=1)
    own, pair = join((own, pair))

    column = {0: own, 1: shifted(own, "z", -1), -1: shifted(own, "z", 1)}
    cot_other = [across(own)]
    for d in range(2, half):
        column[d] = shifted(column[d - 1], "z", -1)
        column[-d] = shifted(column[1 - d], "z", 1)
        if d == half - 1:
            column[1 - d], column[d - 1], cot_other = join((column[1 - d], column[d - 1], cot_other))
        cot_other.insert(0, across(jnp.concatenate([column[d - 1], column[1 - d]], axis=0)))
    before, after = shifted(pair, "fsdp", 1), shifted(pair, "fsdp", -1)
    width = pair.shape[1] // 2
    column, before, after, cot_other = join((column, before, after, cot_other))
    column[half] = shifted(column[1 - half], "z", 1)
    cot_other.insert(0, across(jnp.concatenate([column[half - 1], column[1 - half]], axis=0)))
    far_gate = shifted(before[:, :width], "fsdp", 1)
    far_up = shifted(after[:, width:], "fsdp", -1)
    column, far_gate, far_up, cot_other = join((column, far_gate, far_up, cot_other))
    saved = [pair, before, after, far_gate, far_up]

    cot_mine = [column[d] for d in order]
    cot_other.insert(0, across(column[half]))
    mine_parts, mine_experts = hidden_part(place, cot_mine, down_w, groups)
    mine_got = to_others(mine_parts)
    cot_other, mine_own, x_own = join((cot_other, mine_parts[0], saved_input[0]))
    x_other = across(x_own)
    other_parts, other_experts = hidden_part(place, cot_other, down_w, groups)
    other_got = to_others(other_parts)
    mine_got, other_own, x_own, x_other = join((mine_got, other_parts[0], x_own, x_other))
    x_pair = jnp.where(
        xh == 0,
        jnp.concatenate([x_own, x_other], axis=0),
        jnp.concatenate([x_other, x_own], axis=0),
    )
    x_all = lax.all_gather(x_pair, "z", axis=0, tiled=True)
    mine_grads = spread(summed([mine_own], mine_got))
    experts = [mine_experts, other_experts]
    mine_grads, other_got = join((mine_grads, other_got))
    other_grads = spread(summed([other_own], other_got))
    mine_acts, (part,) = back_part(
        place, mine_ids, mine_experts, mine_grads, saved, gate_w, up_w, 0, (nz,), F32
    )
    other_grads, mine_acts, part = join((other_grads, mine_acts, part))
    early = sum(splits[:2])
    early_acts, early_aways = back_part(
        place, other_ids, other_experts, other_grads, saved, gate_w, up_w, 0, splits[:2], BF16
    )
    first, back = across(early_aways[0]), across(early_aways[1])
    late_acts, aways = back_part(
        place, other_ids, other_experts, other_grads, saved, gate_w, up_w, early, splits[2:], BF16
    )
    first, late_acts, aways = join((first, late_acts, aways))

    def block(rows, i):
        return rows[i * BLOCK : (i + 1) * BLOCK]

    def both(back, at, i):
        return block(part, at) + block(back, i).astype(F32)

    up_sum, down_sum = both(first, 0, 0), None
    for hop in range(half - 1):
        up_sum = shifted(up_sum.astype(BF16), "z", 1)
        if hop:
            down_sum = shifted(down_sum.astype(BF16), "z", -1)
        coming = across(aways[hop]) if hop < len(aways) else None
        if hop == 0:
            gate_grad, up_grad = in_weights(
                ids,
                experts,
                x_all,
                [mine_acts[0], early_acts[0], late_acts[0]],
                [mine_acts[1], early_acts[1], late_acts[1]],
                scale,
            )
            up_sum, back, gate_grad, up_grad = join((up_sum, back, gate_grad, up_grad))
        else:
            up_sum, down_sum, back = join((up_sum, down_sum, back))
        at = 1 + 2 * hop
        up_sum = up_sum.astype(F32) + both(back, at, 0)
        term = both(back, at + 1, 1)
        down_sum = down_sum.astype(F32) + term if hop else term
        if hop == half - 2:
            input_grad = both(back, at + 2, 2)
        back = coming
    up_sum, down_sum = shifted(up_sum, "z", 1), shifted(down_sum, "z", -1)
    down_grad = down_weights(
        place, ids, experts, saved, cot_mine + cot_other, groups, scale
    )
    up_sum, down_sum, down_grad = join((up_sum, down_sum, down_grad))
    input_grad = input_grad + up_sum + down_sum
    return (input_grad.astype(BF16)[None], gate_grad[None], up_grad[None], down_grad[None])


def solution(mesh):
    sizes = mesh.shape
    split = Mesh(
        mesh.devices.reshape(sizes["section"], sizes["dp"] // 2, 2, sizes["fsdp"]),
        ("section", "z", "xh", "fsdp"),
    )
    dp = ("z", "xh")
    rows = P("section", dp, "fsdp")
    kept = P("section", None, ("z", "xh", "fsdp"))
    wide = P("section", None, "fsdp", dp)
    tall = P("section", None, dp, "fsdp")
    return jax.shard_map(
        local,
        mesh=split,
        in_specs=(rows, rows, kept, kept, P("section", dp), wide, wide, tall),
        out_specs=(rows, wide, wide, tall),
        check_vma=False,
    )
```

```python
import functools
import math

import jax
import jax.numpy as jnp
from jax import lax
from jax.experimental import pallas as pl
from jax.experimental.pallas import tpu as pltpu
from jax.sharding import Mesh
from jax.sharding import PartitionSpec as P

E = 2
BLOCK = 128
TAG = 16
VMEM_LIMIT = 60 << 20
NT = (((1,), (1,)), ((), ()))
VM = pl.BlockSpec(memory_space=pltpu.VMEM)
SM = pl.BlockSpec(memory_space=pltpu.SMEM)
F32 = jnp.float32
BF16 = jnp.bfloat16


def shifted(x, axis, by):
    count = lax.axis_size(axis)
    return lax.ppermute(x, axis, [(i, (i + by) % count) for i in range(count)])


def aligned(index, size):
    return pl.ds(pl.multiple_of(index * size, size), size)


def kernel_call(body, out_shape, in_specs, out_specs, scratch, flops, size):
    return pl.pallas_call(
        body,
        out_shape=out_shape,
        in_specs=in_specs,
        out_specs=out_specs,
        scratch_shapes=scratch,
        compiler_params=pltpu.CompilerParams(vmem_limit_bytes=VMEM_LIMIT),
        cost_estimate=pl.CostEstimate(flops=flops, bytes_accessed=size, transcendentals=0),
    )


def piece_of(pieces, j):
    step = BLOCK + TAG
    for piece in pieces:
        held = piece.shape[0] // step
        if j < held:
            start = j * step
            return piece[start : start + BLOCK, :], piece[start + BLOCK : start + step, 0:128]
        j -= held


def hidden_body(count, groups, place_ref, weight_ref, *refs):
    pieces, parts = refs[: -groups - 2], refs[-groups - 2 : -2]
    expert_ref, turned = refs[-2:]
    width = weight_ref.shape[1] // groups
    y = place_ref[0]
    for expert in range(E):
        for k in range(groups):
            turned[expert, k * width : (k + 1) * width, :] = weight_ref[
                expert, aligned(lax.rem(y + k, groups), width), :
            ]
    for j in range(count):
        rows, tag = piece_of(pieces, j)
        expert = jnp.max(tag.astype(F32)).astype(jnp.int32)
        expert_ref[j] = expert
        product = lax.dot_general(
            rows, turned[jnp.minimum(expert, E - 1)], NT, preferred_element_type=F32
        )
        product = product * (expert < E).astype(F32)
        for k in range(groups):
            parts[k][j * BLOCK : (j + 1) * BLOCK, :] = product[
                :, k * width : (k + 1) * width
            ].astype(parts[k].dtype)


def hidden_part(place, pieces, weight, groups):
    count = sum(piece.shape[0] for piece in pieces) // (BLOCK + TAG)
    rows = count * BLOCK
    hidden, cols = weight.shape[1:]
    out_shape = [
        jax.ShapeDtypeStruct((rows, hidden // groups), F32 if k == 0 else BF16)
        for k in range(groups)
    ]
    out_shape.append(jax.ShapeDtypeStruct((count,), jnp.int32))
    outs = kernel_call(
        functools.partial(hidden_body, count, groups),
        out_shape,
        [SM] + [VM] * (len(pieces) + 1),
        [VM] * groups + [SM],
        [pltpu.VMEM(weight.shape, BF16)],
        2 * rows * hidden * cols,
        2 * (rows * cols + E * hidden * cols + rows * hidden),
    )(place, weight, *pieces)
    return outs[:groups], outs[groups]


def saved_pair(saved, k, rows):
    first, second, third, gate_ref, up_ref = saved
    if k == 2:
        gate, up = gate_ref[rows, :].astype(F32), up_ref[rows, :].astype(F32)
    else:
        both = (first, second, None, third)[k][rows, :].astype(F32)
        width = both.shape[1] // 2
        gate, up = both[:, :width], both[:, width:]
    return gate, up, 1.0 / (1.0 + jnp.exp(-gate))


def block_id(order, place_ref, j, other):
    nz = len(order)
    column = 1 - place_ref[2] if other else place_ref[2]
    return lax.rem(place_ref[1] + (order[j] + nz), nz) * 2 + column


def back_body(order, other, first, splits, groups, place_ref, expert_ref, *refs):
    grads, saved = refs[:groups], refs[groups : groups + 5]
    gate_w, up_w, gate_ref, up_ref = refs[groups + 5 : groups + 9]
    outs = refs[groups + 9 :]
    width = grads[0].shape[1]
    y = place_ref[0]
    out_at = [(out, i) for out, blocks in zip(outs, splits) for i in range(blocks)]
    for j, (out, i) in enumerate(out_at):
        rows = slice(j * BLOCK, (j + 1) * BLOCK)
        at = first + j
        saved_rows = aligned(block_id(order, place_ref, at, other), BLOCK)
        for k in range(groups):
            cols = aligned(lax.rem(y + groups - k, groups), width)
            grad = grads[k][at * BLOCK : (at + 1) * BLOCK, :].astype(F32)
            gate, up, sig = saved_pair(saved, k, saved_rows)
            gate_ref[rows, cols] = (grad * up * sig * (1.0 + gate * (1.0 - sig))).astype(BF16)
            up_ref[rows, cols] = (grad * (gate * sig)).astype(BF16)
        chosen = jnp.minimum(expert_ref[at], E - 1)
        share = lax.dot_general(gate_ref[rows, :], gate_w[chosen], NT, preferred_element_type=F32)
        share = share + lax.dot_general(
            up_ref[rows, :], up_w[chosen], NT, preferred_element_type=F32
        )
        out[i * BLOCK : (i + 1) * BLOCK, :] = share.astype(out.dtype)


def back_part(place, order, other, experts, grads, saved, gate_w, up_w, first, splits, kind):
    groups = len(grads)
    rows = sum(splits) * BLOCK
    cols, hidden = gate_w.shape[1:]
    out_shape = [jax.ShapeDtypeStruct((rows, hidden), BF16)] * 2
    out_shape += [jax.ShapeDtypeStruct((blocks * BLOCK, cols), kind) for blocks in splits]
    outs = kernel_call(
        functools.partial(back_body, order, other, first, splits, groups),
        out_shape,
        [SM] * 2 + [VM] * (groups + 7),
        [VM] * len(out_shape),
        [],
        4 * rows * hidden * cols,
        2 * (2 * E * hidden * cols + 6 * rows * hidden + 2 * rows * cols),
    )(place, experts, *grads, *saved, gate_w, up_w)
    return outs[:2], outs[2:]


def weight_body(scale, put, experts, outs, lhs_t, rhs_s, accs):
    slots = sum(ref.shape[0] for ref in experts) + 2
    seen = [jnp.int32(0), jnp.int32(0)]
    for c, ref in enumerate(experts):
        for i in range(ref.shape[0]):
            expert = ref[i]
            slot = jnp.where(expert == 0, seen[0], slots - 1 - seen[1])

            @pl.when(expert < E)
            def _(c=c, i=i, slot=slot):
                put(c, i, aligned(slot, BLOCK))

            seen = [seen[e] + (expert == e).astype(jnp.int32) for e in range(E)]

    for slot, odd in (
        (seen[0], lax.rem(seen[0], 2)),
        (slots - 1 - seen[1], lax.rem(seen[1], 2)),
    ):

        @pl.when(odd == 1)
        def _(slot=slot):
            at = aligned(slot, BLOCK)
            lhs_t[:, at] = jnp.zeros((lhs_t.shape[0], BLOCK), BF16)
            for ref in rhs_s:
                ref[at, :] = jnp.zeros((BLOCK, ref.shape[1]), BF16)

    for expert in range(E):
        for acc in accs:
            acc[...] = jnp.zeros(acc.shape, F32)

        def add(step, carry, expert=expert):
            pair = step if expert == 0 else slots // 2 - 1 - step
            at = aligned(pair, 2 * BLOCK)
            lhs = lhs_t[:, at]
            for acc, rhs in zip(accs, rhs_s):
                acc[...] += jnp.dot(lhs, rhs[at, :], preferred_element_type=F32)
            return carry

        lax.fori_loop(0, lax.div(seen[expert] + 1, 2), add, 0)
        for out, acc in zip(outs, accs):
            out[expert] = (acc[...] * scale).astype(BF16)


def in_weight_body(count, scale, *refs):
    experts, inputs = refs[0:2], refs[2 : 2 + count]
    gates, ups, outs = (refs[at + count : at + count + n] for at, n in ((2, 3), (5, 3), (8, 2)))
    lhs_t, gate_s, up_s, gate_acc, up_acc = refs[-5:]
    early = gates[1].shape[0] // BLOCK

    def put(c, i, at):
        chunk, j = (0, i) if c == 0 else (1, i) if i < early else (2, i - early)
        rows = slice(j * BLOCK, (j + 1) * BLOCK)
        lhs_t[:, at] = inputs[i][c * BLOCK : (c + 1) * BLOCK, :].T
        gate_s[at, :] = gates[chunk][rows, :]
        up_s[at, :] = ups[chunk][rows, :]

    weight_body(scale, put, experts, outs, lhs_t, [gate_s, up_s], [gate_acc, up_acc])


def in_weights(experts, inputs, gates, ups, scale):
    count, cols = len(inputs), inputs[0].shape[1]
    rows = 2 * count * BLOCK
    hidden = gates[0].shape[1]
    wide = rows + 2 * BLOCK
    return kernel_call(
        functools.partial(in_weight_body, count, scale),
        [jax.ShapeDtypeStruct((E, cols, hidden), BF16)] * 2,
        [SM] * 2 + [VM] * (count + 6),
        [VM] * 2,
        [
            pltpu.VMEM((cols, wide), BF16),
            pltpu.VMEM((wide, hidden), BF16),
            pltpu.VMEM((wide, hidden), BF16),
            pltpu.VMEM((cols, hidden), F32),
            pltpu.VMEM((cols, hidden), F32),
        ],
        4 * rows * cols * hidden,
        2 * (rows * cols + 2 * rows * hidden + 2 * E * cols * hidden),
    )(*experts, *inputs, *gates, *ups)


def down_weight_body(order, groups, scale, place_ref, *refs):
    experts, saved, pieces = refs[0:2], refs[2:7], refs[7:-4]
    first = experts[0].shape[0]
    out, lhs_t, rhs_s, acc = refs[-4:]
    width = saved[0].shape[1] // 2
    y = place_ref[0]

    def put(c, i, at):
        rows = aligned(block_id(order, place_ref, i, c == 1), BLOCK)
        for k in range(groups):
            gate, up, sig = saved_pair(saved, k, rows)
            hidden = ((gate * sig) * up).astype(BF16)
            lhs_t[aligned(lax.rem(y + groups - k, groups), width), at] = hidden.T
        rhs_s[at, :] = piece_of(pieces, c * first + i)[0]

    weight_body(scale, put, experts, [out], lhs_t, [rhs_s], [acc])


def down_weights(place, order, experts, saved, pieces, groups, scale):
    rows, cols = saved[0].shape[0], pieces[0].shape[1]
    width = groups * saved[0].shape[1] // 2
    wide = rows + 2 * BLOCK
    return kernel_call(
        functools.partial(down_weight_body, order, groups, scale),
        jax.ShapeDtypeStruct((E, width, cols), BF16),
        [SM] * 3 + [VM] * (5 + len(pieces)),
        VM,
        [
            pltpu.VMEM((width, wide), BF16),
            pltpu.VMEM((wide, cols), BF16),
            pltpu.VMEM((width, cols), F32),
        ],
        2 * rows * cols * width,
        2 * (rows * cols + 2 * rows * width + E * cols * width),
    )(place, *experts, *saved, *pieces)


def local(
    saved_input, pending_grad, gate_pre, up_pre, block_expert, gate_weight, up_weight, down_weight
):
    nz = lax.axis_size("z")
    groups = lax.axis_size("fsdp")
    z, xh, y = lax.axis_index("z"), lax.axis_index("xh"), lax.axis_index("fsdp")
    place = jnp.stack([y, z, xh]).astype(jnp.int32)
    half = nz // 2
    join = lax.optimization_barrier
    across = lambda v: shifted(v, "xh", 1)
    gate_w, up_w, down_w = gate_weight[0], up_weight[0], down_weight[0]
    scale = 1.0 / math.sqrt(saved_input.shape[1] * nz * lax.axis_size("xh"))
    order = (half,) + tuple(s * d for d in range(half - 1, 0, -1) for s in (1, -1)) + (0,)
    splits = (1,) + (2,) * (half - 2) + (3,)

    def summed(parts, got):
        total = parts[0]
        for part in got:
            total = total + part.astype(F32)
        return total

    def to_others(parts):
        return [shifted(parts[k], "fsdp", k) for k in range(1, groups)]

    def spread(total):
        rounded = total.astype(BF16)
        return [total] + to_others([rounded] * groups)

    cotangent = shifted(pending_grad[0], "section", -1)
    tag = jnp.broadcast_to(block_expert.astype(BF16), (TAG, cotangent.shape[1]))
    own = jnp.concatenate([cotangent, tag], axis=0)
    pair = jnp.concatenate([gate_pre[0], up_pre[0]], axis=1)
    own, pair, x_own = join((own, pair, saved_input[0]))
    x_pair = jnp.concatenate([x_own, across(x_own)], axis=0)

    before, after = shifted(pair, "fsdp", 1), shifted(pair, "fsdp", -1)
    width = pair.shape[1] // 2
    column = {0: own, 1: shifted(own, "z", -1), -1: shifted(own, "z", 1)}
    cot_other = [across(own)]
    for d in range(2, half):
        column[d] = shifted(column[d - 1], "z", -1)
        column[-d] = shifted(column[1 - d], "z", 1)
        if d == half - 1:
            column[d], column[-d], cot_other, before, after, x_pair = join(
                (column[d], column[-d], cot_other, before, after, x_pair)
            )
        else:
            column[d], column[-d], cot_other = join((column[d], column[-d], cot_other))
        cot_other.insert(0, across(jnp.concatenate([column[d - 1], column[1 - d]], axis=0)))
    column[half] = shifted(column[1 - half], "z", 1)
    far_gate = shifted(before[:, :width], "fsdp", 1)
    far_up = shifted(after[:, width:], "fsdp", -1)
    column, cot_other = join((column, cot_other))
    cot_other.insert(0, across(jnp.concatenate([column[half - 1], column[1 - half]], axis=0)))

    cot_mine = [column[d] for d in order]
    cot_other.insert(0, across(column[half]))
    mine_parts, mine_experts = hidden_part(place, cot_mine, down_w, groups)
    mine_got = to_others(mine_parts)
    inputs = {0: x_pair, 1: shifted(x_pair, "z", -1), -1: shifted(x_pair, "z", 1)}
    cot_other, mine_own, mine_got, far_gate, far_up, inputs = join(
        (cot_other, mine_parts[0], mine_got, far_gate, far_up, inputs)
    )
    saved = [pair, before, after, far_gate, far_up]
    mine_grads = spread(summed([mine_own], mine_got))
    other_parts, other_experts = hidden_part(place, cot_other, down_w, groups)
    other_got = to_others(other_parts)
    experts = [mine_experts, other_experts]
    inputs[2], inputs[-2] = shifted(inputs[1], "z", -1), shifted(inputs[-1], "z", 1)
    mine_grads, other_own, other_got, inputs = join(
        (mine_grads, other_parts[0], other_got, inputs)
    )
    inputs[3], inputs[-3] = shifted(inputs[2], "z", -1), shifted(inputs[-2], "z", 1)
    other_grads = spread(summed([other_own], other_got))
    mine_acts, (part,) = back_part(
        place, order, False, mine_experts, mine_grads, saved, gate_w, up_w, 0, (nz,), F32
    )
    other_grads, mine_acts, part, inputs = join((other_grads, mine_acts, part, inputs))
    inputs[half] = shifted(inputs[1 - half], "z", 1)
    early = sum(splits[:2])
    early_acts, early_aways = back_part(
        place, order, True, other_experts, other_grads, saved, gate_w, up_w, 0, splits[:2], BF16
    )
    first, back = across(early_aways[0]), across(early_aways[1])
    late_acts, aways = back_part(
        place, order, True, other_experts, other_grads, saved, gate_w, up_w, early, splits[2:], BF16
    )
    first, late_acts, aways, inputs = join((first, late_acts, aways, inputs))

    def block(rows, i):
        return rows[i * BLOCK : (i + 1) * BLOCK]

    def both(back, at, i):
        return block(part, at) + block(back, i).astype(F32)

    up_sum, down_sum = both(first, 0, 0), None
    for hop in range(half - 1):
        up_sum = shifted(up_sum.astype(BF16), "z", 1)
        if hop:
            down_sum = shifted(down_sum.astype(BF16), "z", -1)
        coming = across(aways[hop]) if hop < len(aways) else None
        if hop == 0:
            up_sum, back = join((up_sum, back))
        elif hop == 1:
            up_sum, down_sum, back = join((up_sum, down_sum, back))
        else:
            gate_grad, up_grad = in_weights(
                experts,
                [inputs[d] for d in order],
                [mine_acts[0], early_acts[0], late_acts[0]],
                [mine_acts[1], early_acts[1], late_acts[1]],
                scale,
            )
            up_sum, down_sum, back, gate_grad, up_grad = join(
                (up_sum, down_sum, back, gate_grad, up_grad)
            )
        at = 1 + 2 * hop
        up_sum = up_sum.astype(F32) + both(back, at, 0)
        term = both(back, at + 1, 1)
        down_sum = down_sum.astype(F32) + term if hop else term
        if hop == half - 2:
            input_grad = both(back, at + 2, 2)
        back = coming
    up_sum, down_sum = shifted(up_sum, "z", 1), shifted(down_sum, "z", -1)
    down_grad = down_weights(
        place, order, experts, saved, cot_mine + cot_other, groups, scale
    )
    up_sum, down_sum, down_grad = join((up_sum, down_sum, down_grad))
    input_grad = input_grad + up_sum + down_sum
    return (input_grad.astype(BF16)[None], gate_grad[None], up_grad[None], down_grad[None])


def solution(mesh):
    sizes = mesh.shape
    split = Mesh(
        mesh.devices.reshape(sizes["section"], sizes["dp"] // 2, 2, sizes["fsdp"]),
        ("section", "z", "xh", "fsdp"),
    )
    dp = ("z", "xh")
    rows = P("section", dp, "fsdp")
    kept = P("section", None, ("z", "xh", "fsdp"))
    wide = P("section", None, "fsdp", dp)
    tall = P("section", None, dp, "fsdp")
    return jax.shard_map(
        local,
        mesh=split,
        in_specs=(rows, rows, kept, kept, P("section", dp), wide, wide, tall),
        out_specs=(rows, wide, wide, tall),
        check_vma=False,
    )
```

```python
import functools
import math

import jax
import jax.numpy as jnp
from jax import lax
from jax.experimental import pallas as pl
from jax.experimental.pallas import tpu as pltpu
from jax.sharding import Mesh
from jax.sharding import PartitionSpec as P

E = 2
BLOCK = 128
TAG = 16
VMEM_LIMIT = 60 << 20
NT = (((1,), (1,)), ((), ()))
VM = pl.BlockSpec(memory_space=pltpu.VMEM)
SM = pl.BlockSpec(memory_space=pltpu.SMEM)
F32 = jnp.float32
BF16 = jnp.bfloat16


def shifted(x, axis, by):
    count = lax.axis_size(axis)
    return lax.ppermute(x, axis, [(i, (i + by) % count) for i in range(count)])


def aligned(index, size):
    return pl.ds(pl.multiple_of(index * size, size), size)


def kernel_call(body, out_shape, in_specs, out_specs, scratch, flops, size):
    return pl.pallas_call(
        body,
        out_shape=out_shape,
        in_specs=in_specs,
        out_specs=out_specs,
        scratch_shapes=scratch,
        compiler_params=pltpu.CompilerParams(vmem_limit_bytes=VMEM_LIMIT),
        cost_estimate=pl.CostEstimate(flops=flops, bytes_accessed=size, transcendentals=0),
    )


def piece_of(pieces, j):
    step = BLOCK + TAG
    for piece in pieces:
        held = piece.shape[0] // step
        if j < held:
            start = j * step
            return piece[start : start + BLOCK, :], piece[start + BLOCK : start + step, 0:128]
        j -= held


def hidden_body(count, groups, place_ref, weight_ref, *refs):
    pieces, parts = refs[: -groups - 2], refs[-groups - 2 : -2]
    expert_ref, turned = refs[-2:]
    width = weight_ref.shape[1] // groups
    y = place_ref[0]
    for expert in range(E):
        for k in range(groups):
            turned[expert, k * width : (k + 1) * width, :] = weight_ref[
                expert, aligned(lax.rem(y + k, groups), width), :
            ]
    for j in range(count):
        rows, tag = piece_of(pieces, j)
        expert = jnp.max(tag.astype(F32)).astype(jnp.int32)
        expert_ref[j] = expert
        product = lax.dot_general(
            rows, turned[jnp.minimum(expert, E - 1)], NT, preferred_element_type=F32
        )
        product = product * (expert < E).astype(F32)
        for k in range(groups):
            parts[k][j * BLOCK : (j + 1) * BLOCK, :] = product[
                :, k * width : (k + 1) * width
            ].astype(parts[k].dtype)


def hidden_part(place, pieces, weight, groups):
    count = sum(piece.shape[0] for piece in pieces) // (BLOCK + TAG)
    rows = count * BLOCK
    hidden, cols = weight.shape[1:]
    out_shape = [
        jax.ShapeDtypeStruct((rows, hidden // groups), F32 if k == 0 else BF16)
        for k in range(groups)
    ]
    out_shape.append(jax.ShapeDtypeStruct((count,), jnp.int32))
    outs = kernel_call(
        functools.partial(hidden_body, count, groups),
        out_shape,
        [SM] + [VM] * (len(pieces) + 1),
        [VM] * groups + [SM],
        [pltpu.VMEM(weight.shape, BF16)],
        2 * rows * hidden * cols,
        2 * (rows * cols + E * hidden * cols + rows * hidden),
    )(place, weight, *pieces)
    return outs[:groups], outs[groups]


def saved_pair(saved, k, rows):
    first, second, third, gate_ref, up_ref = saved
    if k == 2:
        gate, up = gate_ref[rows, :].astype(F32), up_ref[rows, :].astype(F32)
    else:
        both = (first, second, None, third)[k][rows, :].astype(F32)
        width = both.shape[1] // 2
        gate, up = both[:, :width], both[:, width:]
    return gate, up, 1.0 / (1.0 + jnp.exp(-gate))


def block_id(order, place_ref, j, other):
    nz = len(order)
    column = 1 - place_ref[2] if other else place_ref[2]
    return lax.rem(place_ref[1] + (order[j] + nz), nz) * 2 + column


def back_body(order, other, first, splits, groups, place_ref, expert_ref, *refs):
    grads, saved = refs[:groups], refs[groups : groups + 5]
    gate_w, up_w, gate_ref, up_ref = refs[groups + 5 : groups + 9]
    outs = refs[groups + 9 :]
    width = grads[0].shape[1]
    y = place_ref[0]
    out_at = [(out, i) for out, blocks in zip(outs, splits) for i in range(blocks)]
    for j, (out, i) in enumerate(out_at):
        rows = slice(j * BLOCK, (j + 1) * BLOCK)
        at = first + j
        saved_rows = aligned(block_id(order, place_ref, at, other), BLOCK)
        for k in range(groups):
            cols = aligned(lax.rem(y + groups - k, groups), width)
            grad = grads[k][at * BLOCK : (at + 1) * BLOCK, :].astype(F32)
            gate, up, sig = saved_pair(saved, k, saved_rows)
            gate_ref[rows, cols] = (grad * up * sig * (1.0 + gate * (1.0 - sig))).astype(BF16)
            up_ref[rows, cols] = (grad * (gate * sig)).astype(BF16)
        chosen = jnp.minimum(expert_ref[at], E - 1)
        share = lax.dot_general(gate_ref[rows, :], gate_w[chosen], NT, preferred_element_type=F32)
        share = share + lax.dot_general(
            up_ref[rows, :], up_w[chosen], NT, preferred_element_type=F32
        )
        out[i * BLOCK : (i + 1) * BLOCK, :] = share.astype(out.dtype)


def back_part(place, order, other, experts, grads, saved, gate_w, up_w, first, splits, kind):
    groups = len(grads)
    rows = sum(splits) * BLOCK
    cols, hidden = gate_w.shape[1:]
    out_shape = [jax.ShapeDtypeStruct((rows, hidden), BF16)] * 2
    out_shape += [jax.ShapeDtypeStruct((blocks * BLOCK, cols), kind) for blocks in splits]
    outs = kernel_call(
        functools.partial(back_body, order, other, first, splits, groups),
        out_shape,
        [SM] * 2 + [VM] * (groups + 7),
        [VM] * len(out_shape),
        [],
        4 * rows * hidden * cols,
        2 * (2 * E * hidden * cols + 6 * rows * hidden + 2 * rows * cols),
    )(place, experts, *grads, *saved, gate_w, up_w)
    return outs[:2], outs[2:]


def weight_body(scale, put, experts, outs, lhs_t, rhs_s, accs):
    slots = sum(ref.shape[0] for ref in experts) + 2
    seen = [jnp.int32(0), jnp.int32(0)]
    for c, ref in enumerate(experts):
        for i in range(ref.shape[0]):
            expert = ref[i]
            slot = jnp.where(expert == 0, seen[0], slots - 1 - seen[1])

            @pl.when(expert < E)
            def _(c=c, i=i, slot=slot):
                put(c, i, aligned(slot, BLOCK))

            seen = [seen[e] + (expert == e).astype(jnp.int32) for e in range(E)]

    for slot, odd in (
        (seen[0], lax.rem(seen[0], 2)),
        (slots - 1 - seen[1], lax.rem(seen[1], 2)),
    ):

        @pl.when(odd == 1)
        def _(slot=slot):
            at = aligned(slot, BLOCK)
            lhs_t[:, at] = jnp.zeros((lhs_t.shape[0], BLOCK), BF16)
            for ref in rhs_s:
                ref[at, :] = jnp.zeros((BLOCK, ref.shape[1]), BF16)

    for expert in range(E):
        for acc in accs:
            acc[...] = jnp.zeros(acc.shape, F32)

        def add(step, carry, expert=expert):
            pair = step if expert == 0 else slots // 2 - 1 - step
            at = aligned(pair, 2 * BLOCK)
            lhs = lhs_t[:, at]
            for acc, rhs in zip(accs, rhs_s):
                acc[...] += jnp.dot(lhs, rhs[at, :], preferred_element_type=F32)
            return carry

        lax.fori_loop(0, lax.div(seen[expert] + 1, 2), add, 0)
        for out, acc in zip(outs, accs):
            out[expert] = (acc[...] * scale).astype(BF16)


def in_weight_body(count, scale, *refs):
    experts, inputs = refs[0:2], refs[2 : 2 + count]
    gates, ups, outs = (refs[at + count : at + count + n] for at, n in ((2, 3), (5, 3), (8, 2)))
    lhs_t, gate_s, up_s, gate_acc, up_acc = refs[-5:]
    early = gates[1].shape[0] // BLOCK

    def put(c, i, at):
        chunk, j = (0, i) if c == 0 else (1, i) if i < early else (2, i - early)
        rows = slice(j * BLOCK, (j + 1) * BLOCK)
        lhs_t[:, at] = inputs[i][c * BLOCK : (c + 1) * BLOCK, :].T
        gate_s[at, :] = gates[chunk][rows, :]
        up_s[at, :] = ups[chunk][rows, :]

    weight_body(scale, put, experts, outs, lhs_t, [gate_s, up_s], [gate_acc, up_acc])


def in_weights(experts, inputs, gates, ups, scale):
    count, cols = len(inputs), inputs[0].shape[1]
    rows = 2 * count * BLOCK
    hidden = gates[0].shape[1]
    wide = rows + 2 * BLOCK
    return kernel_call(
        functools.partial(in_weight_body, count, scale),
        [jax.ShapeDtypeStruct((E, cols, hidden), BF16)] * 2,
        [SM] * 2 + [VM] * (count + 6),
        [VM] * 2,
        [
            pltpu.VMEM((cols, wide), BF16),
            pltpu.VMEM((wide, hidden), BF16),
            pltpu.VMEM((wide, hidden), BF16),
            pltpu.VMEM((cols, hidden), F32),
            pltpu.VMEM((cols, hidden), F32),
        ],
        4 * rows * cols * hidden,
        2 * (rows * cols + 2 * rows * hidden + 2 * E * cols * hidden),
    )(*experts, *inputs, *gates, *ups)


def down_weight_body(order, groups, scale, place_ref, *refs):
    experts, saved, pieces = refs[0:2], refs[2:7], refs[7:-4]
    first = experts[0].shape[0]
    out, lhs_t, rhs_s, acc = refs[-4:]
    width = saved[0].shape[1] // 2
    y = place_ref[0]

    def put(c, i, at):
        rows = aligned(block_id(order, place_ref, i, c == 1), BLOCK)
        for k in range(groups):
            gate, up, sig = saved_pair(saved, k, rows)
            hidden = ((gate * sig) * up).astype(BF16)
            lhs_t[aligned(lax.rem(y + groups - k, groups), width), at] = hidden.T
        rhs_s[at, :] = piece_of(pieces, c * first + i)[0]

    weight_body(scale, put, experts, [out], lhs_t, [rhs_s], [acc])


def down_weights(place, order, experts, saved, pieces, groups, scale):
    rows, cols = saved[0].shape[0], pieces[0].shape[1]
    width = groups * saved[0].shape[1] // 2
    wide = rows + 2 * BLOCK
    return kernel_call(
        functools.partial(down_weight_body, order, groups, scale),
        jax.ShapeDtypeStruct((E, width, cols), BF16),
        [SM] * 3 + [VM] * (5 + len(pieces)),
        VM,
        [
            pltpu.VMEM((width, wide), BF16),
            pltpu.VMEM((wide, cols), BF16),
            pltpu.VMEM((width, cols), F32),
        ],
        2 * rows * cols * width,
        2 * (rows * cols + 2 * rows * width + E * cols * width),
    )(place, *experts, *saved, *pieces)


def local(
    saved_input, pending_grad, gate_pre, up_pre, block_expert, gate_weight, up_weight, down_weight
):
    nz = lax.axis_size("z")
    groups = lax.axis_size("fsdp")
    z, xh, y = lax.axis_index("z"), lax.axis_index("xh"), lax.axis_index("fsdp")
    place = jnp.stack([y, z, xh]).astype(jnp.int32)
    half = nz // 2
    join = lax.optimization_barrier
    across = lambda v: shifted(v, "xh", 1)
    gate_w, up_w, down_w = gate_weight[0], up_weight[0], down_weight[0]
    scale = 1.0 / math.sqrt(saved_input.shape[1] * nz * lax.axis_size("xh"))
    order = (half,) + tuple(s * d for d in range(half - 1, 0, -1) for s in (1, -1)) + (0,)
    splits = (1,) + (2,) * (half - 2) + (3,)

    def summed(parts, got):
        total = parts[0]
        for part in got:
            total = total + part.astype(F32)
        return total

    def to_others(parts):
        return [shifted(parts[k], "fsdp", k) for k in range(1, groups)]

    def spread(total):
        rounded = total.astype(BF16)
        return [total] + to_others([rounded] * groups)

    cotangent = shifted(pending_grad[0], "section", -1)
    tag = jnp.broadcast_to(block_expert.astype(BF16), (TAG, cotangent.shape[1]))
    own = jnp.concatenate([cotangent, tag], axis=0)
    pair = jnp.concatenate([gate_pre[0], up_pre[0]], axis=1)
    own, pair, x_own = join((own, pair, saved_input[0]))
    x_pair = jnp.concatenate([x_own, across(x_own)], axis=0)

    before, after = shifted(pair, "fsdp", 1), shifted(pair, "fsdp", -1)
    width = pair.shape[1] // 2
    column = {0: own, 1: shifted(own, "z", -1), -1: shifted(own, "z", 1)}
    cot_other = [across(own)]
    for d in range(2, half):
        column[d] = shifted(column[d - 1], "z", -1)
        column[-d] = shifted(column[1 - d], "z", 1)
        if d == half - 1:
            column[d], column[-d], cot_other, before, after, x_pair = join(
                (column[d], column[-d], cot_other, before, after, x_pair)
            )
        else:
            column[d], column[-d], cot_other = join((column[d], column[-d], cot_other))
        cot_other.insert(0, across(jnp.concatenate([column[d - 1], column[1 - d]], axis=0)))
    column[half] = shifted(column[1 - half], "z", 1)
    far_gate = shifted(before[:, :width], "fsdp", 1)
    far_up = shifted(after[:, width:], "fsdp", -1)
    column, cot_other = join((column, cot_other))
    cot_other.insert(0, across(jnp.concatenate([column[half - 1], column[1 - half]], axis=0)))

    cot_mine = [column[d] for d in order]
    cot_other.insert(0, across(column[half]))
    mine_parts, mine_experts = hidden_part(place, cot_mine, down_w, groups)
    mine_got = to_others(mine_parts)
    inputs = {0: x_pair, 1: shifted(x_pair, "z", -1), -1: shifted(x_pair, "z", 1)}
    cot_other, mine_own, far_gate, far_up, inputs = join(
        (cot_other, mine_parts[0], far_gate, far_up, inputs)
    )
    saved = [pair, before, after, far_gate, far_up]
    other_parts, other_experts = hidden_part(place, cot_other, down_w, groups)
    other_got = to_others(other_parts)
    experts = [mine_experts, other_experts]
    inputs[2], inputs[-2] = shifted(inputs[1], "z", -1), shifted(inputs[-1], "z", 1)
    mine_got, other_own, inputs = join((mine_got, other_parts[0], inputs))
    inputs[3], inputs[-3] = shifted(inputs[2], "z", -1), shifted(inputs[-2], "z", 1)
    mine_grads = spread(summed([mine_own], mine_got))
    mine_grads, other_got, inputs = join((mine_grads, other_got, inputs))
    inputs[half] = shifted(inputs[1 - half], "z", 1)
    other_grads = spread(summed([other_own], other_got))
    mine_acts, (part,) = back_part(
        place, order, False, mine_experts, mine_grads, saved, gate_w, up_w, 0, (nz,), F32
    )
    other_grads, mine_acts, part, inputs = join((other_grads, mine_acts, part, inputs))
    early = sum(splits[:2])
    early_acts, early_aways = back_part(
        place, order, True, other_experts, other_grads, saved, gate_w, up_w, 0, splits[:2], BF16
    )
    first, back = across(early_aways[0]), across(early_aways[1])
    late_acts, aways = back_part(
        place, order, True, other_experts, other_grads, saved, gate_w, up_w, early, splits[2:], BF16
    )
    first, late_acts, aways, inputs = join((first, late_acts, aways, inputs))

    def block(rows, i):
        return rows[i * BLOCK : (i + 1) * BLOCK]

    def both(back, at, i):
        return block(part, at) + block(back, i).astype(F32)

    up_sum, down_sum = both(first, 0, 0), None
    for hop in range(half - 1):
        up_sum = shifted(up_sum.astype(BF16), "z", 1)
        if hop:
            down_sum = shifted(down_sum.astype(BF16), "z", -1)
        coming = across(aways[hop]) if hop < len(aways) else None
        if hop == 0:
            up_sum, back = join((up_sum, back))
        elif hop == 1:
            up_sum, down_sum, back = join((up_sum, down_sum, back))
        else:
            gate_grad, up_grad = in_weights(
                experts,
                [inputs[d] for d in order],
                [mine_acts[0], early_acts[0], late_acts[0]],
                [mine_acts[1], early_acts[1], late_acts[1]],
                scale,
            )
            up_sum, down_sum, back, gate_grad, up_grad = join(
                (up_sum, down_sum, back, gate_grad, up_grad)
            )
        at = 1 + 2 * hop
        up_sum = up_sum.astype(F32) + both(back, at, 0)
        term = both(back, at + 1, 1)
        down_sum = down_sum.astype(F32) + term if hop else term
        if hop == half - 2:
            input_grad = both(back, at + 2, 2)
        back = coming
    up_sum, down_sum = shifted(up_sum, "z", 1), shifted(down_sum, "z", -1)
    down_grad = down_weights(
        place, order, experts, saved, cot_mine + cot_other, groups, scale
    )
    up_sum, down_sum, down_grad = join((up_sum, down_sum, down_grad))
    input_grad = input_grad + up_sum + down_sum
    return (input_grad.astype(BF16)[None], gate_grad[None], up_grad[None], down_grad[None])


def solution(mesh):
    sizes = mesh.shape
    split = Mesh(
        mesh.devices.reshape(sizes["section"], sizes["dp"] // 2, 2, sizes["fsdp"]),
        ("section", "z", "xh", "fsdp"),
    )
    dp = ("z", "xh")
    rows = P("section", dp, "fsdp")
    kept = P("section", None, ("z", "xh", "fsdp"))
    wide = P("section", None, "fsdp", dp)
    tall = P("section", None, dp, "fsdp")
    return jax.shard_map(
        local,
        mesh=split,
        in_specs=(rows, rows, kept, kept, P("section", dp), wide, wide, tall),
        out_specs=(rows, wide, wide, tall),
        check_vma=False,
    )
```
